32 devices in a mesh: row: 8 (over y, x, core), col: 4 (over z).
Axes of the slice: x: 2, y: 2, z: 4, core: 2. Of those that a mesh axis runs over, the one named last changes fastest.
Arguments:
- row_emb: float32 [32, 300, 1024], P(('row', 'col')), may hold values from -1.5 to 1.5
- col_emb: float32 [32, 300, 1024], P(('row', 'col')), may hold values from -1.5 to 1.5
- row_acc: float32 [32, 300, 1024], P(('row', 'col')), may hold values from 0.5 to 8
- col_acc: float32 [32, 300, 1024], P(('row', 'col')), may hold values from 0.5 to 8
- marginal_log: float32 [32768], replicated, may hold values from -2 to 1
- tile_rows: int32 [96], P(('row', 'col')), may hold values from 0 to 31, as said below
- tile_cols: int32 [96], P(('row', 'col')), may hold values from 0 to 31, as said below
- counts: int32 [96, 1024, 1024], P(('row', 'col')), may hold values from 0 to 2047
Outputs:
- new_row_emb: float32 [32, 300, 1024], P(('row', 'col'))
- new_col_emb: float32 [32, 300, 1024], P(('row', 'col'))
- new_row_acc: float32 [32, 300, 1024], P(('row', 'col'))
- new_col_acc: float32 [32, 300, 1024], P(('row', 'col'))
The draws below stay inside these ranges and needn't reach their ends.
Inputs may be any that keep to these rules, and one draw needn't show every extreme that they name: Block g of the embeddings lies on device g in the mesh's order (row slowest). Slot k lies on device p = k // 3; with p at row index r and col index c, tile_rows[k] // 4 equals r. With slot k on the device at col index c, tile_cols[k] % 4 equals c.
All inputs are finite; a program needn't handle non-finite values.
Results may differ from the reference program's by a relative error of at most 0.019.
Values may be sent and summed in bfloat16 or wider, within the bound.
A program may use at most 128 MiB of HBM per device.

```python
import math
import jax
import jax.numpy as jnp
from jax import lax

D = 300
BLOCK = 1024
TILES_DEV = 3
NBLK = 32
TILES = 96
WORDS = 32768
N_ROW = 8
N_COL = 4


def pick_skewed(key, choices_total, shape_tuple):
    ranks = jnp.arange(choices_total, dtype=jnp.int32)
    weights = jnp.maximum(1, 64 // (ranks + 1))
    bounds = jnp.cumsum(weights)
    picks = jax.random.randint(key, shape_tuple, 0, bounds[-1])
    rank_of = jnp.sum((picks[..., None] >= bounds).astype(jnp.int32), axis=-1)
    ordering = jax.random.permutation(jax.random.fold_in(key, 7), choices_total)
    return ordering[rank_of].astype(jnp.int32)


def draw_tile_rows(key, part):
    slots = jnp.arange(TILES, dtype=jnp.int32)
    device = slots // TILES_DEV
    row_index = device // N_COL
    chosen = pick_skewed(jax.random.fold_in(key, 11), N_COL, (TILES,))
    return (row_index * N_COL + chosen).astype(jnp.int32)


def draw_tile_cols(key, part):
    slots = jnp.arange(TILES, dtype=jnp.int32)
    device = slots // TILES_DEV
    col_index = device % N_COL
    chosen = pick_skewed(jax.random.fold_in(key, 13), N_ROW, (TILES,))
    return (chosen * N_COL + col_index).astype(jnp.int32)


def draw_counts(key, part):
    shape_tuple = (TILES, BLOCK, BLOCK)
    present = jax.random.randint(jax.random.fold_in(key, 21), shape_tuple, 0, 5) >= 2
    level = jax.random.randint(jax.random.fold_in(key, 22), shape_tuple, 0, 12)
    raw_bits = jax.random.randint(jax.random.fold_in(key, 23), shape_tuple, 0, 1 << 20)
    values = 1 + raw_bits % jnp.left_shift(jnp.ones(shape_tuple, jnp.int32), level)
    values = jnp.minimum(values, 2047)
    return jnp.where(present, values, 0).astype(jnp.int32)


def block_levels(key, shape, split, smallest, top_value):
    def one(axis_at, parts):
        draws = jax.random.uniform(jax.random.fold_in(jax.random.fold_in(key, 6), axis_at), (parts,), jnp.float32, smallest / len(split), top_value / len(split))
        return jnp.repeat(jnp.exp(draws), shape[axis_at] // parts).reshape((-1,) + (1,) * (len(shape) - axis_at - 1))

    gain = one(*split[0])
    for cut in split[1:]:
        gain = gain * one(*cut)
    return gain


def normal_values(own_key, dims, spread, reach, shards=(), kind=jnp.bfloat16):
    values = spread * jax.random.normal(own_key, dims, jnp.float32)
    if shards:
        values = values * block_levels(own_key, dims, shards, -0.22, 0.18)
    return jnp.clip(values, -reach, reach).astype(kind)


def setup_inputs(seed: int = 0) -> dict:
    key_list = jax.random.split(jax.random.key(seed), 9)
    row_emb = normal_values(key_list[0], (NBLK, D, BLOCK), 0.25, 1.5, ((0, 32),), jnp.float32)
    col_emb = normal_values(key_list[1], (NBLK, D, BLOCK), 0.25, 1.5, ((0, 32),), jnp.float32)
    row_acc = jnp.clip(jnp.exp(math.log(8.0) - 2.7725887 * jax.random.uniform(key_list[2], (NBLK, D, BLOCK), jnp.float32) ** block_levels(key_list[2], (NBLK, D, BLOCK), ((0, 32),), -0.2, 0.2)), 0.5, 8.0)
    col_acc = jnp.clip(jnp.exp(math.log(8.0) - 2.7725887 * jax.random.uniform(key_list[3], (NBLK, D, BLOCK), jnp.float32) ** block_levels(key_list[3], (NBLK, D, BLOCK), ((0, 32),), -0.2, 0.2)), 0.5, 8.0)
    marginal_log = jnp.clip(jax.random.uniform(key_list[4], (WORDS,), jnp.float32, -2.0, 1.0), -2.0, 1.0)
    tile_rows = draw_tile_rows(jax.random.fold_in(key_list[8], 71), 0)
    tile_cols = draw_tile_cols(jax.random.fold_in(key_list[8], 71), 0)
    counts = draw_counts(jax.random.fold_in(key_list[8], 71), 0)
    return dict(row_emb=row_emb, col_emb=col_emb, row_acc=row_acc, col_acc=col_acc, marginal_log=marginal_log, tile_rows=tile_rows, tile_cols=tile_cols, counts=counts)


err_scale = 0.03125
learn_rate = 0.1

def tile_terms(row_block, col_block, tile_counts, row_margin, col_margin):
    scores = lax.dot_general(row_block, col_block, (((0,), (0,)), ((), ())), preferred_element_type=jnp.float32)
    counted = tile_counts.astype(jnp.float32)
    shifted_log = jnp.log(jnp.maximum(counted, 1.0)) - row_margin[:, None] - col_margin[None, :]
    residue = scores - shifted_log
    weighted = (0.1 + 0.25 * jnp.sqrt(counted)) * residue
    cell_grad = jnp.where(tile_counts > 0, weighted, jax.nn.sigmoid(residue)) * err_scale
    errors = cell_grad.astype(jnp.bfloat16)
    row_term = lax.dot_general(col_block, errors, (((1,), (1,)), ((), ())), preferred_element_type=jnp.float32)
    col_term = jnp.dot(row_block, errors, preferred_element_type=jnp.float32)
    return (row_term, col_term)

def add_slot(buffer, slot_index, term):
    old_value = lax.dynamic_index_in_dim(buffer, slot_index, 0, keepdims=False)
    return lax.dynamic_update_index_in_dim(buffer, old_value + term, slot_index, 0)

def adagrad(weights, history, gradient):
    grown = history + gradient * gradient
    return (weights - learn_rate * gradient / jnp.sqrt(grown), grown)

def reference(row_emb, col_emb, row_acc, col_acc, marginal_log, tile_rows, tile_cols, counts):
    row_low = row_emb.astype(jnp.bfloat16)
    col_low = col_emb.astype(jnp.bfloat16)
    col_grid = col_low.reshape(N_ROW, N_COL, D, BLOCK)
    zeros_table = jnp.zeros((NBLK, D, BLOCK), jnp.float32)

    def device_step(tables, device):
        row_table, col_table = tables
        row_index = (device // N_COL).astype(jnp.int32)
        col_index = (device % N_COL).astype(jnp.int32)
        rows_near = lax.dynamic_slice_in_dim(row_low, row_index * N_COL, N_COL, 0)
        cols_near = lax.dynamic_index_in_dim(col_grid, col_index, 1, keepdims=False)
        row_part = jnp.zeros((N_COL, D, BLOCK), jnp.float32)
        col_part = jnp.zeros((N_ROW, D, BLOCK), jnp.float32)
        for tile_slot in range(TILES_DEV):
            position = (device * TILES_DEV + tile_slot).astype(jnp.int32)
            row_id = lax.dynamic_index_in_dim(tile_rows, position, 0, keepdims=False).astype(jnp.int32)
            col_id = lax.dynamic_index_in_dim(tile_cols, position, 0, keepdims=False).astype(jnp.int32)
            row_slot = (row_id - row_index * N_COL).astype(jnp.int32)
            col_slot = (col_id // N_COL).astype(jnp.int32)
            row_block = lax.dynamic_index_in_dim(rows_near, row_slot, 0, keepdims=False)
            col_block = lax.dynamic_index_in_dim(cols_near, col_slot, 0, keepdims=False)
            tile_counts = lax.dynamic_index_in_dim(counts, position, 0, keepdims=False)
            row_margin = lax.dynamic_slice_in_dim(marginal_log, (row_id * BLOCK).astype(jnp.int32), BLOCK)
            col_margin = lax.dynamic_slice_in_dim(marginal_log, (col_id * BLOCK).astype(jnp.int32), BLOCK)
            row_term, col_term = tile_terms(row_block, col_block, tile_counts, row_margin, col_margin)
            row_part = add_slot(row_part, row_slot, row_term)
            col_part = add_slot(col_part, col_slot, col_term)
        row_round = lax.optimization_barrier(row_part.astype(jnp.bfloat16)).astype(jnp.float32)
        col_round = lax.optimization_barrier(col_part.astype(jnp.bfloat16)).astype(jnp.float32)
        old_rows = lax.dynamic_slice_in_dim(row_table, row_index * N_COL, N_COL, 0)
        row_table = lax.dynamic_update_slice_in_dim(row_table, old_rows + row_round, row_index * N_COL, 0)
        col_gridded = col_table.reshape(N_ROW, N_COL, D, BLOCK)
        old_cols = lax.dynamic_index_in_dim(col_gridded, col_index, 1, keepdims=False)
        col_gridded = lax.dynamic_update_index_in_dim(col_gridded, old_cols + col_round, col_index, 1)
        return ((row_table, col_gridded.reshape(NBLK, D, BLOCK)), None)
    sums_pair, unused = lax.scan(device_step, (zeros_table, zeros_table), jnp.arange(NBLK, dtype=jnp.int32))
    row_grad, col_grad = sums_pair
    new_row_emb, new_row_acc = adagrad(row_emb, row_acc, row_grad)
    new_col_emb, new_col_acc = adagrad(col_emb, col_acc, col_grad)
    return (new_row_emb, new_col_emb, new_row_acc, new_col_acc)
```

```python
import functools

import jax
import jax.numpy as jnp
from jax import lax
from jax.experimental import pallas as pl
from jax.experimental.pallas import tpu as pltpu
from jax.sharding import PartitionSpec as P

err_scale = 0.03125
learn_rate = 0.1
chunk_count = 4
count_slots = 4
MESH = pl.DeviceIdType.MESH


def flip(index, mask):
    bit = 1
    while bit <= mask:
        if mask & bit:
            index = index + bit * (1 - 2 * ((index // bit) % 2))
        bit *= 2
    return index


def step_kernel(n_row, n_col, tiles, row_slots, col_slots, row_pick, col_pick, row_in, col_in,
                counts, row_out, col_out, *scratch):
    nc = chunk_count
    rows_near = scratch[:nc]
    row_send = scratch[nc:2 * nc]
    row_recv = scratch[2 * nc:3 * nc]
    (cols_near, col_part, sib_recv, peer_recv, count_buf, row_term, col_term,
     z_send, z_recv, c_send, c_recv, s_send, s_recv, cnt_sem, rs_send, rs_recv,
     q_send, q_recv, p_send, p_recv) = scratch[3 * nc:]
    chips = n_row // 2
    block_len = row_in.shape[1]
    width = block_len // nc
    r = lax.axis_index("row")
    i = lax.axis_index("col")
    q = r // 2
    core = r % 2
    sib = flip(r, 1)
    has_left = i > 0
    has_right = i < n_col - 1

    def row_dev(index):
        return (index, i)

    def col_dev(index):
        return (r, index)

    def count_copy(piece):
        c, t = piece // tiles, piece % tiles
        return pltpu.make_async_copy(
            counts.at[t, pl.ds(pl.multiple_of(c * width, width), width), :],
            count_buf.at[piece % count_slots], cnt_sem.at[piece % count_slots])

    for piece in range(count_slots):
        count_copy(piece).start()

    for c in range(nc):
        rows_near[c][i] = row_in[:, c * width:(c + 1) * width]
    cols_near[r] = col_in[...]

    barrier = pltpu.get_barrier_semaphore()
    for m in range(1, chips):
        pl.semaphore_signal(barrier, inc=1, device_id=row_dev(2 * flip(q, m) + core), device_id_type=MESH)
    pl.semaphore_signal(barrier, inc=1, device_id=row_dev(sib), device_id_type=MESH)

    @pl.when(has_left)
    def _():
        pl.semaphore_signal(barrier, inc=1, device_id=col_dev(i - 1), device_id_type=MESH)

    @pl.when(has_right)
    def _():
        pl.semaphore_signal(barrier, inc=1, device_id=col_dev(i + 1), device_id_type=MESH)

    pl.semaphore_wait(barrier, chips + jnp.minimum(i, 1) + jnp.minimum(n_col - 1 - i, 1))

    def z_copy(c, block, way):
        return pltpu.make_async_remote_copy(
            src_ref=rows_near[c].at[block], dst_ref=rows_near[c].at[block],
            send_sem=z_send.at[way, c, block], recv_sem=z_recv.at[c, block],
            device_id=col_dev(i + 1 - 2 * way), device_id_type=MESH)

    def z_own(c):
        @pl.when(has_right)
        def _():
            z_copy(c, i, 0).start()

        @pl.when(has_left)
        def _():
            z_copy(c, i, 1).start()

    def z_forward(c):
        for s in range(1, n_col):
            @pl.when(i - s >= 0)
            def _():
                z_copy(c, i - s, 0).wait_recv()

                @pl.when(has_right)
                def _():
                    z_copy(c, i - s, 0).start()

            @pl.when(i + s < n_col)
            def _():
                z_copy(c, i + s, 1).wait_recv()

                @pl.when(has_left)
                def _():
                    z_copy(c, i + s, 1).start()

    def z_drain(c):
        for block in range(n_col):
            @pl.when(has_right & (block <= i))
            def _():
                z_copy(c, block, 0).wait_send()

            @pl.when(has_left & (block >= i))
            def _():
                z_copy(c, block, 1).wait_send()

    def col_copy(m, block):
        return pltpu.make_async_remote_copy(
            src_ref=cols_near.at[block], dst_ref=cols_near.at[block],
            send_sem=c_send.at[m], recv_sem=c_recv.at[block // 2],
            device_id=row_dev(2 * flip(q, m) + core), device_id_type=MESH)

    def sib_copy(block):
        return pltpu.make_async_remote_copy(
            src_ref=cols_near.at[block], dst_ref=cols_near.at[block],
            send_sem=s_send.at[block // 2], recv_sem=s_recv.at[block // 2],
            device_id=row_dev(sib), device_id_type=MESH)

    def col_arrive(m):
        block = 2 * flip(q, m) + core
        col_copy(m, block).wait_recv()
        sib_copy(block).start()

    z_own(0)
    for m in reversed(range(1, chips)):
        col_copy(m, r).start()
    sib_copy(r).start()
    z_own(1)

    masks = list(range(1, chips))
    z_next = 0
    for at, m in enumerate(masks):
        if z_next < nc - 1 and at < nc - 1:
            z_forward(z_next)
            if z_next + 2 < nc:
                z_own(z_next + 2)
            z_next += 1
        col_arrive(m)
    for chip in range(chips):
        sib_copy(2 * chip + 1 - core).wait_recv()

    def row_copy(c, j, way, slot):
        return pltpu.make_async_remote_copy(
            src_ref=row_send[c].at[j], dst_ref=row_recv[c].at[slot],
            send_sem=rs_send.at[c, j], recv_sem=rs_recv.at[c, slot],
            device_id=col_dev(i + 1 - 2 * way), device_id_type=MESH)

    def row_pass(c):
        for s in range(1, n_col):
            far = n_col - s

            @pl.when(i - far >= 0)
            def _():
                j = i - far

                @pl.when(has_right)
                def _():
                    row_copy(c, j, 1, j).wait_recv()
                    row_send[c][j] = row_send[c][j] + row_recv[c][j]

                row_copy(c, j, 1, n_col if far == 1 else j).start()

            @pl.when(i + far < n_col)
            def _():
                j = i + far

                @pl.when(has_left)
                def _():
                    row_copy(c, j, 0, j).wait_recv()
                    row_send[c][j] = row_send[c][j] + row_recv[c][j]

                row_copy(c, j, 0, j).start()

    def row_finish(c):
        span = slice(c * width, (c + 1) * width)
        row_out[:, span] = row_send[c][i].astype(jnp.float32)

        @pl.when(has_left)
        def _():
            row_copy(c, i, 0, i).wait_recv()
            row_out[:, span] += row_recv[c][i].astype(jnp.float32)

        @pl.when(has_right)
        def _():
            row_copy(c, i, 1, n_col).wait_recv()
            row_out[:, span] += row_recv[c][n_col].astype(jnp.float32)

        for j in range(n_col):
            @pl.when(j != i)
            def _():
                row_copy(c, j, 0, j).wait_send()

    def compute(c):
        def one_tile(t, carry):
            piece = c * tiles + t
            row_block = rows_near[c][row_slots[t]]
            col_block = cols_near[col_slots[t]]
            count_copy(piece).wait()
            raw = count_buf[piece % count_slots]

            scores = lax.dot_general(
                row_block, col_block, (((0,), (0,)), ((), ())), preferred_element_type=jnp.float32)
            counted = jnp.maximum(raw, 1).astype(jnp.float32)
            residue = scores - jnp.log(counted)
            weighted = (0.1 * err_scale + 0.25 * err_scale * (counted * lax.rsqrt(counted))) * residue
            soft = 0.5 * err_scale * jnp.tanh(0.5 * residue) + 0.5 * err_scale
            errors = jnp.where(raw > 0, weighted, soft).astype(jnp.bfloat16)
            row_term[t] = lax.dot_general(
                col_block, errors, (((1,), (1,)), ((), ())), preferred_element_type=jnp.float32)
            grown = jnp.dot(row_block, errors, preferred_element_type=jnp.float32)
            if c == 0:
                col_term[t] = grown
            else:
                col_term[t] += grown

            @pl.when(piece + count_slots < nc * tiles)
            def _():
                count_copy(piece + count_slots).start()

            return carry

        lax.fori_loop(0, tiles, one_tile, 0)

        def one_dest(j, carry):
            total = row_term[0] * row_pick[j]
            for t in range(1, tiles):
                total += row_term[t] * row_pick[t * n_col + j]
            row_send[c][j] = total.astype(jnp.bfloat16)
            return carry

        lax.fori_loop(0, n_col, one_dest, 0)

    for c in range(nc):
        if c == z_next:
            z_forward(c)
            z_next += 1
            if c + 2 < nc:
                z_own(c + 2)
        compute(c)
        if z_next < nc and z_next == c + 1:
            z_forward(z_next)
            if z_next + 2 < nc:
                z_own(z_next + 2)
            z_next += 1
        if c > 0:
            row_pass(c - 1)

    def col_total(d):
        total = col_term[0] * col_pick[d]
        for t in range(1, tiles):
            total += col_term[t] * col_pick[t * n_row + d]
        return total.astype(jnp.bfloat16)

    def sib_sum(chip):
        return pltpu.make_async_remote_copy(
            src_ref=col_part.at[2 * chip + 1 - core], dst_ref=sib_recv.at[chip],
            send_sem=q_send.at[chip], recv_sem=q_recv.at[chip],
            device_id=row_dev(sib), device_id_type=MESH)

    def peer_sum(m):
        chip = flip(q, m)
        return pltpu.make_async_remote_copy(
            src_ref=col_part.at[2 * chip + core], dst_ref=peer_recv.at[m],
            send_sem=p_send.at[m], recv_sem=p_recv.at[m],
            device_id=row_dev(2 * chip + core), device_id_type=MESH)

    order = list(reversed(range(1, chips))) + [0]
    for m in order:
        chip = flip(q, m)
        col_part[2 * chip + 1 - core] = col_total(2 * chip + 1 - core)
        sib_sum(chip).start()
    row_pass(nc - 1)
    for m in order:
        chip = flip(q, m)
        mine = 2 * chip + core
        col_part[mine] = col_total(mine)
        sib_sum(chip).wait_recv()
        if m > 0:
            col_part[mine] = col_part[mine] + sib_recv[chip]
            peer_sum(m).start()
    col_out[...] = col_part[r].astype(jnp.float32) + sib_recv[q].astype(jnp.float32)

    for c in range(nc):
        row_finish(c)
    for m in range(1, chips):
        peer_sum(m).wait_recv()
        col_out[...] += peer_recv[m].astype(jnp.float32)

    for c in range(nc):
        z_drain(c)
    for m in range(1, chips):
        col_copy(m, r).wait_send()
        peer_sum(m).wait_send()
    for chip in range(chips):
        sib_copy(2 * chip + core).wait_send()
        sib_sum(chip).wait_send()


def adagrad(weights, history, gradient):
    grown = history + gradient * gradient
    return (weights - learn_rate * gradient / jnp.sqrt(grown), grown)


def body(row_emb, col_emb, row_acc, col_acc, marginal_log, tile_rows, tile_cols, counts):
    n_col = lax.axis_size("col")
    n_row = lax.axis_size("row")
    emb_width, block_len = row_emb.shape[1:]
    tiles = counts.shape[0]
    chips = n_row // 2
    nc = chunk_count
    width = block_len // nc
    me = lax.axis_index("row") * n_col + lax.axis_index("col")
    margin = lax.dynamic_slice_in_dim(marginal_log, me * block_len, block_len)
    high = lax.reduce_precision(margin, 8, 7)
    pair = jnp.stack([high, margin - high]).astype(jnp.bfloat16)
    padded = -(-(emb_width + 4) // 16) * 16
    ones = jnp.ones((2, block_len), jnp.bfloat16)
    zeros = jnp.zeros((padded - emb_width - 4, block_len), jnp.bfloat16)
    row_in = jnp.concatenate([row_emb[0].astype(jnp.bfloat16), pair, ones, zeros])
    col_in = jnp.concatenate([col_emb[0].astype(jnp.bfloat16), ones, pair, zeros])
    row_slots = tile_rows % n_col
    col_slots = tile_cols // n_col
    row_pick = (row_slots[:, None] == jnp.arange(n_col)[None, :]).astype(jnp.float32).reshape(-1)
    col_pick = (col_slots[:, None] == jnp.arange(n_row)[None, :]).astype(jnp.float32).reshape(-1)

    smem = pl.BlockSpec(memory_space=pltpu.SMEM)
    vmem = pl.BlockSpec(memory_space=pltpu.VMEM)
    bf16 = jnp.bfloat16
    dma = pltpu.SemaphoreType.DMA
    scratch = (
        [pltpu.VMEM((n_col, padded, width), bf16)] * nc
        + [pltpu.VMEM((n_col, padded, width), bf16)] * nc
        + [pltpu.VMEM((n_col + 1, padded, width), bf16)] * nc
        + [
            pltpu.VMEM((n_row, padded, block_len), bf16),
            pltpu.VMEM((n_row, padded, block_len), bf16),
            pltpu.VMEM((chips, padded, block_len), bf16),
            pltpu.VMEM((chips, padded, block_len), bf16),
            pltpu.VMEM((count_slots, width, block_len), jnp.int32),
            pltpu.VMEM((tiles, padded, width), jnp.float32),
            pltpu.VMEM((tiles, padded, block_len), jnp.float32),
            dma((2, nc, n_col)), dma((nc, n_col)),
            dma((chips,)), dma((chips,)), dma((chips,)), dma((chips,)),
            dma((count_slots,)),
            dma((nc, n_col)), dma((nc, n_col + 1)),
            dma((chips,)), dma((chips,)), dma((chips,)), dma((chips,)),
        ]
    )
    row_sum, col_sum = pl.pallas_call(
        functools.partial(step_kernel, n_row, n_col, tiles),
        out_shape=[jax.ShapeDtypeStruct((padded, block_len), jnp.float32)] * 2,
        in_specs=[smem] * 4 + [vmem] * 2 + [pl.BlockSpec(memory_space=pl.ANY)],
        out_specs=[vmem] * 2,
        scratch_shapes=scratch,
        compiler_params=pltpu.CompilerParams(
            collective_id=0, has_side_effects=True, vmem_limit_bytes=62 * 1024 * 1024),
    )(row_slots, col_slots, row_pick, col_pick, row_in, col_in, counts)
    new_row_emb, new_row_acc = adagrad(row_emb, row_acc, row_sum[None, :emb_width])
    new_col_emb, new_col_acc = adagrad(col_emb, col_acc, col_sum[None, :emb_width])
    return (new_row_emb, new_col_emb, new_row_acc, new_col_acc)


def solution(mesh):
    blocks = P(("row", "col"), None, None)
    listed = P(("row", "col"))
    return jax.shard_map(
        body,
        mesh=mesh,
        in_specs=(blocks, blocks, blocks, blocks, P(), listed, listed, blocks),
        out_specs=(blocks, blocks, blocks, blocks),
        check_vma=False,
    )
```

```python
import functools

import jax
import jax.numpy as jnp
from jax import lax
from jax.experimental import pallas as pl
from jax.experimental.pallas import tpu as pltpu
from jax.sharding import PartitionSpec as P

err_scale = 0.03125
learn_rate = 0.1
chunk_count = 4
count_slots = 4
MESH = pl.DeviceIdType.MESH


def flip(index, mask):
    bit = 1
    while bit <= mask:
        if mask & bit:
            index = index + bit * (1 - 2 * ((index // bit) % 2))
        bit *= 2
    return index


def step_kernel(n_row, n_col, tiles, tile_rows, tile_cols, row_in, col_in,
                counts, row_out, col_out, *scratch):
    nc = chunk_count
    rows_near = scratch[:nc]
    row_send = scratch[nc:2 * nc]
    row_recv = scratch[2 * nc:3 * nc]
    (cols_near, col_part, sib_recv, peer_recv, count_buf, row_term, col_term,
     z_send, z_recv, c_send, c_recv, s_send, s_recv, cnt_sem, rs_send, rs_recv,
     q_send, q_recv, p_send, p_recv) = scratch[3 * nc:]
    chips = n_row // 2
    block_len = row_in.shape[1]
    width = block_len // nc
    half = -(-row_in.shape[0] // 32) * 16
    r = lax.axis_index("row")
    i = lax.axis_index("col")
    q = r // 2
    core = r % 2
    sib = flip(r, 1)
    has_left = i > 0
    has_right = i < n_col - 1

    def row_dev(index):
        return (index, i)

    def col_dev(index):
        return (r, index)

    def count_copy(piece):
        c, t = piece // tiles, piece % tiles
        return pltpu.make_async_copy(
            counts.at[t, pl.ds(pl.multiple_of(c * width, width), width), :],
            count_buf.at[piece % count_slots], cnt_sem.at[piece % count_slots])

    for piece in range(count_slots):
        count_copy(piece).start()

    for c in range(nc):
        rows_near[c][i] = row_in[:, c * width:(c + 1) * width]
    cols_near[r] = col_in[...]

    barrier = pltpu.get_barrier_semaphore()
    for m in range(1, chips):
        pl.semaphore_signal(barrier, inc=1, device_id=row_dev(2 * flip(q, m) + core), device_id_type=MESH)
    pl.semaphore_signal(barrier, inc=1, device_id=row_dev(sib), device_id_type=MESH)

    @pl.when(has_left)
    def _():
        pl.semaphore_signal(barrier, inc=1, device_id=col_dev(i - 1), device_id_type=MESH)

    @pl.when(has_right)
    def _():
        pl.semaphore_signal(barrier, inc=1, device_id=col_dev(i + 1), device_id_type=MESH)

    pl.semaphore_wait(barrier, chips + jnp.minimum(i, 1) + jnp.minimum(n_col - 1 - i, 1))

    def z_copy(c, block, way):
        return pltpu.make_async_remote_copy(
            src_ref=rows_near[c].at[block], dst_ref=rows_near[c].at[block],
            send_sem=z_send.at[way, c, block], recv_sem=z_recv.at[c, block],
            device_id=col_dev(i + 1 - 2 * way), device_id_type=MESH)

    def z_own(c):
        @pl.when(has_right)
        def _():
            z_copy(c, i, 0).start()

        @pl.when(has_left)
        def _():
            z_copy(c, i, 1).start()

    def z_forward(c):
        for s in range(1, n_col):
            @pl.when(i - s >= 0)
            def _():
                z_copy(c, i - s, 0).wait_recv()

                @pl.when(has_right)
                def _():
                    z_copy(c, i - s, 0).start()

            @pl.when(i + s < n_col)
            def _():
                z_copy(c, i + s, 1).wait_recv()

                @pl.when(has_left)
                def _():
                    z_copy(c, i + s, 1).start()

    def z_drain(c):
        for block in range(n_col):
            @pl.when(has_right & (block <= i))
            def _():
                z_copy(c, block, 0).wait_send()

            @pl.when(has_left & (block >= i))
            def _():
                z_copy(c, block, 1).wait_send()

    def col_copy(m, block):
        return pltpu.make_async_remote_copy(
            src_ref=cols_near.at[block], dst_ref=cols_near.at[block],
            send_sem=c_send.at[m], recv_sem=c_recv.at[block // 2],
            device_id=row_dev(2 * flip(q, m) + core), device_id_type=MESH)

    def sib_copy(block):
        return pltpu.make_async_remote_copy(
            src_ref=cols_near.at[block], dst_ref=cols_near.at[block],
            send_sem=s_send.at[block // 2], recv_sem=s_recv.at[block // 2],
            device_id=row_dev(sib), device_id_type=MESH)

    def col_arrive(m):
        block = 2 * flip(q, m) + core
        col_copy(m, block).wait_recv()
        sib_copy(block).start()

    z_own(0)
    for m in reversed(range(1, chips)):
        col_copy(m, r).start()
    sib_copy(r).start()
    z_own(1)

    masks = list(range(1, chips))
    z_next = 0
    for at, m in enumerate(masks):
        if z_next < nc - 1 and at < nc - 1:
            z_forward(z_next)
            if z_next + 2 < nc:
                z_own(z_next + 2)
            z_next += 1
        col_arrive(m)
    for chip in range(chips):
        sib_copy(2 * chip + 1 - core).wait_recv()

    def row_copy(c, j, way, slot):
        return pltpu.make_async_remote_copy(
            src_ref=row_send[c].at[j], dst_ref=row_recv[c].at[slot],
            send_sem=rs_send.at[c, j], recv_sem=rs_recv.at[c, slot],
            device_id=col_dev(i + 1 - 2 * way), device_id_type=MESH)

    def row_pass(c):
        for s in range(1, n_col):
            far = n_col - s

            @pl.when(i - far >= 0)
            def _():
                j = i - far

                @pl.when(has_right)
                def _():
                    row_copy(c, j, 1, j).wait_recv()
                    row_send[c][j] = row_send[c][j] + row_recv[c][j]

                row_copy(c, j, 1, n_col if far == 1 else j).start()

            @pl.when(i + far < n_col)
            def _():
                j = i + far

                @pl.when(has_left)
                def _():
                    row_copy(c, j, 0, j).wait_recv()
                    row_send[c][j] = row_send[c][j] + row_recv[c][j]

                row_copy(c, j, 0, j).start()

    def row_finish(c):
        span = slice(c * width, (c + 1) * width)
        row_out[:, span] = row_send[c][i].astype(jnp.float32)

        @pl.when(has_left)
        def _():
            row_copy(c, i, 0, i).wait_recv()
            row_out[:, span] += row_recv[c][i].astype(jnp.float32)

        @pl.when(has_right)
        def _():
            row_copy(c, i, 1, n_col).wait_recv()
            row_out[:, span] += row_recv[c][n_col].astype(jnp.float32)

        for j in range(n_col):
            @pl.when(j != i)
            def _():
                row_copy(c, j, 0, j).wait_send()

    def compute(c):
        def one_tile(t, carry):
            piece = c * tiles + t
            row_block = rows_near[c][tile_rows[t] % n_col]
            col_block = cols_near[tile_cols[t] // n_col]
            count_copy(piece).wait()
            raw = count_buf[piece % count_slots]

            scores = lax.dot_general(
                row_block, col_block, (((0,), (0,)), ((), ())), preferred_element_type=jnp.float32)
            counted = jnp.maximum(raw, 1).astype(jnp.float32)
            residue = scores - jnp.log(counted)
            weighted = (0.1 * err_scale + 0.25 * err_scale * (counted * lax.rsqrt(counted))) * residue
            soft = 0.5 * err_scale * jnp.tanh(0.5 * residue) + 0.5 * err_scale
            errors = jnp.where(raw > 0, weighted, soft).astype(jnp.bfloat16)
            row_term[t] = lax.dot_general(
                col_block, errors, (((1,), (1,)), ((), ())), preferred_element_type=jnp.float32)
            grown = jnp.dot(row_block, errors, preferred_element_type=jnp.float32)
            if c == 0:
                col_term[t] = grown
            else:
                col_term[t] += grown

            @pl.when(piece + count_slots < nc * tiles)
            def _():
                count_copy(piece + count_slots).start()

            return carry

        lax.fori_loop(0, tiles, one_tile, 0)

        def one_dest(j, carry):
            total = jnp.where(tile_rows[0] % n_col == j, row_term[0], 0.0)
            for t in range(1, tiles):
                total += jnp.where(tile_rows[t] % n_col == j, row_term[t], 0.0)
            row_send[c][j] = total.astype(jnp.bfloat16)
            return carry

        lax.fori_loop(0, n_col, one_dest, 0)

    for c in range(nc):
        if c == z_next:
            z_forward(c)
            z_next += 1
            if c + 2 < nc:
                z_own(c + 2)
        compute(c)
        if z_next < nc and z_next == c + 1:
            z_forward(z_next)
            if z_next + 2 < nc:
                z_own(z_next + 2)
            z_next += 1
        if c > 0:
            row_pass(c - 1)

    def col_total(d):
        total = jnp.where(tile_cols[0] // n_col == d, col_term[0], 0.0)
        for t in range(1, tiles):
            total += jnp.where(tile_cols[t] // n_col == d, col_term[t], 0.0)
        return total.astype(jnp.bfloat16)

    def sib_sum(chip):
        return pltpu.make_async_remote_copy(
            src_ref=col_part.at[2 * chip + 1 - core], dst_ref=sib_recv.at[chip],
            send_sem=q_send.at[chip], recv_sem=q_recv.at[chip],
            device_id=row_dev(sib), device_id_type=MESH)

    def peer_sum(m):
        chip = flip(q, m)
        return pltpu.make_async_remote_copy(
            src_ref=col_part.at[2 * chip + core], dst_ref=peer_recv.at[m],
            send_sem=p_send.at[m], recv_sem=p_recv.at[m],
            device_id=row_dev(2 * chip + core), device_id_type=MESH)

    order = list(reversed(range(1, chips))) + [0]
    for m in order:
        chip = flip(q, m)
        col_part[2 * chip + 1 - core] = col_total(2 * chip + 1 - core)
        sib_sum(chip).start()

    def col_own(m):
        chip = flip(q, m)
        mine = 2 * chip + core
        total = col_total(mine)
        sib_sum(chip).wait_recv()
        if m > 0:
            total = total + sib_recv[chip]
        col_part[mine] = total

    if chips == 4:
        diag = 2 * flip(q, 3) + core
        near_x, near_y = 2 * flip(q, 1) + core, 2 * flip(q, 2) + core

        def half_sum(span, m, sem):
            return pltpu.make_async_remote_copy(
                src_ref=col_part.at[diag, span], dst_ref=peer_recv.at[0, span],
                send_sem=p_send.at[sem], recv_sem=p_recv.at[sem],
                device_id=row_dev(2 * flip(q, m) + core), device_id_type=MESH)

        low, high = pl.ds(0, half), pl.ds(half, col_in.shape[0] - half)
        col_own(3)
        half_sum(low, 1, 0).start()
        half_sum(high, 2, 3).start()
        col_own(1)
        col_own(2)
        half_sum(high, 2, 3).wait_recv()
        col_part[near_x, high] = col_part[near_x, high] + peer_recv[0, high]
        peer_sum(1).start()
        half_sum(low, 1, 0).wait_recv()
        col_part[near_y, low] = col_part[near_y, low] + peer_recv[0, low]
        peer_sum(2).start()
        last = [1, 2]
    else:
        for m in order[:-1]:
            col_own(m)
            peer_sum(m).start()
        last = list(range(1, chips))
    row_pass(nc - 1)
    col_own(0)
    col_out[...] = col_part[r].astype(jnp.float32) + sib_recv[q].astype(jnp.float32)

    for c in range(nc):
        row_finish(c)
    for m in last:
        peer_sum(m).wait_recv()
        col_out[...] += peer_recv[m].astype(jnp.float32)

    for c in range(nc):
        z_drain(c)
    for m in range(1, chips):
        col_copy(m, r).wait_send()
    for m in last:
        peer_sum(m).wait_send()
    if chips == 4:
        half_sum(low, 1, 0).wait_send()
        half_sum(high, 2, 3).wait_send()
    for chip in range(chips):
        sib_copy(2 * chip + core).wait_send()
        sib_sum(chip).wait_send()


def adagrad(weights, history, gradient):
    grown = history + gradient * gradient
    return (weights - learn_rate * gradient / jnp.sqrt(grown), grown)


def body(row_emb, col_emb, row_acc, col_acc, marginal_log, tile_rows, tile_cols, counts):
    n_col = lax.axis_size("col")
    n_row = lax.axis_size("row")
    emb_width, block_len = row_emb.shape[1:]
    tiles = counts.shape[0]
    chips = n_row // 2
    nc = chunk_count
    width = block_len // nc
    me = lax.axis_index("row") * n_col + lax.axis_index("col")
    margin = lax.dynamic_slice_in_dim(marginal_log, me * block_len, block_len)
    high = lax.reduce_precision(margin, 8, 7)
    pair = jnp.stack([high, margin - high]).astype(jnp.bfloat16)
    padded = -(-(emb_width + 4) // 16) * 16
    ones = jnp.ones((2, block_len), jnp.bfloat16)
    zeros = jnp.zeros((padded - emb_width - 4, block_len), jnp.bfloat16)
    row_in = jnp.concatenate([row_emb[0].astype(jnp.bfloat16), pair, ones, zeros])
    col_in = jnp.concatenate([col_emb[0].astype(jnp.bfloat16), ones, pair, zeros])
    smem = pl.BlockSpec(memory_space=pltpu.SMEM)
    vmem = pl.BlockSpec(memory_space=pltpu.VMEM)
    bf16 = jnp.bfloat16
    dma = pltpu.SemaphoreType.DMA
    scratch = (
        [pltpu.VMEM((n_col, padded, width), bf16)] * nc
        + [pltpu.VMEM((n_col, padded, width), bf16)] * nc
        + [pltpu.VMEM((n_col + 1, padded, width), bf16)] * nc
        + [
            pltpu.VMEM((n_row, padded, block_len), bf16),
            pltpu.VMEM((n_row, padded, block_len), bf16),
            pltpu.VMEM((chips, padded, block_len), bf16),
            pltpu.VMEM((chips, padded, block_len), bf16),
            pltpu.VMEM((count_slots, width, block_len), jnp.int32),
            pltpu.VMEM((tiles, padded, width), jnp.float32),
            pltpu.VMEM((tiles, padded, block_len), jnp.float32),
            dma((2, nc, n_col)), dma((nc, n_col)),
            dma((chips,)), dma((chips,)), dma((chips,)), dma((chips,)),
            dma((count_slots,)),
            dma((nc, n_col)), dma((nc, n_col + 1)),
            dma((chips,)), dma((chips,)), dma((chips,)), dma((chips,)),
        ]
    )
    row_sum, col_sum = pl.pallas_call(
        functools.partial(step_kernel, n_row, n_col, tiles),
        out_shape=[jax.ShapeDtypeStruct((padded, block_len), jnp.float32)] * 2,
        in_specs=[smem] * 2 + [vmem] * 2 + [pl.BlockSpec(memory_space=pl.ANY)],
        out_specs=[vmem] * 2,
        scratch_shapes=scratch,
        compiler_params=pltpu.CompilerParams(
            collective_id=0, has_side_effects=True, vmem_limit_bytes=62 * 1024 * 1024),
    )(tile_rows, tile_cols, row_in, col_in, counts)
    def flat(block):
        return lax.optimization_barrier(block.reshape(-1, 128))

    rows = adagrad(flat(row_emb), flat(row_acc), flat(row_sum[:emb_width]))
    cols = adagrad(flat(col_emb), flat(col_acc), flat(col_sum[:emb_width]))
    ordered = lax.optimization_barrier((rows[0], cols[0], rows[1], cols[1]))
    return tuple(out.reshape(row_emb.shape) for out in ordered)


def solution(mesh):
    blocks = P(("row", "col"), None, None)
    listed = P(("row", "col"))
    return jax.shard_map(
        body,
        mesh=mesh,
        in_specs=(blocks, blocks, blocks, blocks, P(), listed, listed, blocks),
        out_specs=(blocks, blocks, blocks, blocks),
        check_vma=False,
    )
```
